256 devices in a mesh: dp: 32 (over z_hi, x, core), tensor: 8 (over z_lo, y).
Axes of the slice: x: 4, y: 4, z: 8 (z_hi: 4, z_lo: 2; z = z_hi * 2 + z_lo), core: 2. Of those that a mesh axis runs over, the one named last changes fastest.
Arguments:
- gate_pre: bfloat16 [4096, 14336], P('dp', 'tensor'), may hold values from -6 to 6
- up_pre: bfloat16 [4096, 14336], P('dp', 'tensor'), may hold values from -6 to 6
- out_grad: bfloat16 [4096, 8192], P('dp', 'tensor'), may hold values from -5 to 5, as said below
- other_sq: float32 [64], P('dp'), may hold values from 0.0625 to 0.5
- added_noise: bfloat16 [8192, 14336], P('dp', 'tensor'), may hold values from -0.59765625 to 0.59765625
Outputs:
- down_grad: float32 [8192, 14336], P('dp', 'tensor')
- clip_factor: float32 [64], P('dp')
The draws below stay inside these ranges and needn't reach their ends.
Inputs may be any that keep to these rules, and one draw needn't show every extreme that they name: `out_grad`: each example's rows share one scale.
All inputs are finite; a program needn't handle non-finite values.
Results may differ from the reference program's by a relative error of at most 0.0016.
Values may be sent and summed in bfloat16 or wider, within the bound.
No kernel may reach another device: no remote copies, remote signals or barrier semaphores. Data moves between devices by JAX's collectives and lax.ppermute only.
A program may use at most 128 MiB of HBM per device.

```python
import math
import jax
import jax.numpy as jnp
from jax import lax

D = 8192
FF = 14336
TOK_EX = 64
EXAMPLES = 64


def topic_loadings(key):
    load_key = jax.random.fold_in(key, 101)
    weight_key = jax.random.fold_in(key, 102)
    loadings = 0.8 + 0.6 * jax.random.normal(load_key, (EXAMPLES, TOK_EX, 4), jnp.float32)
    strength = jax.random.uniform(weight_key, (EXAMPLES, 1, 1), jnp.float32, 0.5, 1.5)
    return (loadings, strength)


def blend_topics(dir_key, noise_part, loadings, strength):
    feature_count = noise_part.shape[2]
    directions = jax.random.normal(dir_key, (EXAMPLES, 4, feature_count), jnp.float32)
    shared = jnp.zeros_like(noise_part)
    for topic_index in range(4):
        shared = shared + loadings[:, :, topic_index:topic_index + 1] * directions[:, topic_index:topic_index + 1, :]
    return (noise_part + strength * 0.5 * shared) / jnp.sqrt(1.0 + strength * strength)


def draw_gate_pre(key, part):
    loadings, strength = topic_loadings(key)
    key = jax.random.fold_in(key, 11)
    dir_key, noise_key = jax.random.split(key)
    noise_part = jax.random.normal(noise_key, (EXAMPLES, TOK_EX, FF), jnp.float32)
    values = jnp.clip(blend_topics(dir_key, noise_part, loadings, strength), -6.0, 6.0)
    return values.reshape(EXAMPLES * TOK_EX, FF).astype(jnp.bfloat16)


def draw_up_pre(key, part):
    loadings, strength = topic_loadings(key)
    key = jax.random.fold_in(key, 13)
    dir_key, noise_key = jax.random.split(key)
    noise_part = jax.random.normal(noise_key, (EXAMPLES, TOK_EX, FF), jnp.float32)
    values = jnp.clip(blend_topics(dir_key, noise_part, loadings, strength), -6.0, 6.0)
    return values.reshape(EXAMPLES * TOK_EX, FF).astype(jnp.bfloat16)


def draw_out_grad(key, part):
    loadings, strength = topic_loadings(key)
    key = jax.random.fold_in(key, 7)
    first_key, second_key, third_key = jax.random.split(key, 3)
    scales = jnp.exp(jax.random.uniform(first_key, (EXAMPLES, 1, 1), jnp.float32, jnp.log(0.25), jnp.log(4.0)))
    noise_part = jax.random.normal(second_key, (EXAMPLES, TOK_EX, D), jnp.float32)
    values = blend_topics(third_key, noise_part, loadings, strength)
    values = jnp.clip(values * scales / jnp.sqrt(jnp.float32(TOK_EX)), -5.0, 5.0)
    return values.reshape(EXAMPLES * TOK_EX, D).astype(jnp.bfloat16)


def block_scale(rng, shape, pieces, least, top_value):
    def one(dim, parts):
        draws = jax.random.uniform(jax.random.fold_in(jax.random.fold_in(rng, 6), dim), (parts,), jnp.float32, least / len(pieces), top_value / len(pieces))
        return jnp.repeat(jnp.exp(draws), shape[dim] // parts).reshape((-1,) + (1,) * (len(shape) - dim - 1))

    level = one(*pieces[0])
    for cut in pieces[1:]:
        level = level * one(*cut)
    return level


def bell_draw(key, extent, spread, bound, pieces=(), kind=jnp.bfloat16):
    drawn = spread * jax.random.normal(key, extent, jnp.float32)
    if pieces:
        drawn = drawn * block_scale(key, extent, pieces, -0.22, 0.18)
    return jnp.clip(drawn, -bound, bound).astype(kind)


def setup_inputs(seed: int = 0) -> dict:
    streams_of = jax.random.split(jax.random.key(seed), 6)
    gate_pre = draw_gate_pre(jax.random.fold_in(streams_of[5], 71), 0)
    up_pre = draw_up_pre(jax.random.fold_in(streams_of[5], 71), 0)
    out_grad = draw_out_grad(jax.random.fold_in(streams_of[5], 71), 0)
    other_sq = jnp.clip(jnp.exp(math.log(0.5) - 2.0794415 * jax.random.uniform(streams_of[3], (EXAMPLES,), jnp.float32) ** block_scale(streams_of[3], (EXAMPLES,), ((0, 32),), -0.2, 0.2)), 0.0625, 0.5)
    added_noise = bell_draw(streams_of[4], (D, FF), 0.1, 0.59765625, ((0, 32), (1, 8)))
    return dict(gate_pre=gate_pre, up_pre=up_pre, out_grad=out_grad, other_sq=other_sq, added_noise=added_noise)


def reference(gate_pre, up_pre, out_grad, other_sq, added_noise):
    hidden = (jax.nn.silu(gate_pre.astype(jnp.float32)) * up_pre.astype(jnp.float32)).astype(jnp.bfloat16)
    hidden_blocks = hidden.reshape(EXAMPLES, TOK_EX, FF).astype(jnp.float32)
    grad_blocks = out_grad.reshape(EXAMPLES, TOK_EX, D).astype(jnp.float32)
    hidden_gram = jnp.einsum('btf,buf->btu', hidden_blocks, hidden_blocks)
    grad_gram = jnp.einsum('btf,buf->btu', grad_blocks, grad_blocks)
    down_sq = lax.optimization_barrier(jnp.sum(hidden_gram * grad_gram, axis=(1, 2)))
    weight_count = jnp.float32(D) * jnp.float32(FF)
    clip_factor = jnp.minimum(jnp.float32(1.0), jnp.float32(1.0) / jnp.sqrt(down_sq / weight_count + other_sq))
    token_factor = jnp.repeat(clip_factor, TOK_EX)
    scaled = (token_factor[:, None] * out_grad.astype(jnp.float32)).astype(jnp.bfloat16)
    summed = jnp.dot(scaled.T, hidden, preferred_element_type=jnp.float32)
    down_grad = summed / jnp.float32(EXAMPLES) + added_noise.astype(jnp.float32)
    return (down_grad, clip_factor)
```

```python
import jax
import jax.numpy as jnp
from jax import lax
from jax.experimental import pallas as pl
from jax.experimental.pallas import tpu as pltpu
from jax.sharding import PartitionSpec as P

D = 8192
FF = 14336

DEVICES = [
    (zh, x, c, zl, y)
    for zh in range(4)
    for x in range(4)
    for c in range(2)
    for zl in range(2)
    for y in range(4)
]


def index(zh, x, c, zl, y):
    return (((zh % 4) * 4 + x % 4) * 2 + c % 2) * 8 + (zl % 2) * 4 + y % 4


def send(value, zh=0, x=0, c=0, zl=0, y=0):
    pairs = [
        (index(*d), index(d[0] + zh, d[1] + x, d[2] + c, d[3] + zl, d[4] + y)) for d in DEVICES
    ]
    return lax.ppermute(value, ("dp", "tensor"), pairs)


def pick(stacked, at):
    return lax.dynamic_index_in_dim(stacked, at, 0, keepdims=False)


def matmul_kernel(layout, *refs):
    scaled_ref, *piece_refs = refs[:-1]
    out_ref = refs[-1]
    for start, stop, blocks in layout:
        for lo in range(start, stop, 256):
            hi = min(lo + 256, stop)
            rows = [piece_refs[p][:, lo - off : hi - off] for p, off in blocks]
            out_ref[:, lo:hi] = jnp.dot(
                scaled_ref[...], jnp.concatenate(rows, axis=0), preferred_element_type=jnp.float32
            )


def per_device(gate_pre, up_pre, out_grad, other_sq, added_noise):
    dp_at, t_at = lax.axis_index("dp"), lax.axis_index("tensor")
    zh_at, x_at, c_at = dp_at // 8, (dp_at // 2) % 4, dp_at % 2
    zl_at, y_at = t_at // 4, t_at % 4
    tok, ff = gate_pre.shape
    examples = 64
    ex = 2

    hidden = (jax.nn.silu(gate_pre.astype(jnp.float32)) * up_pre.astype(jnp.float32)).astype(
        jnp.bfloat16
    )
    half = ff // 2
    a, b = 384, ff - 384
    pieces = {(0, 0): [(0, hidden)]}
    pieces[1, 0] = [(0, send(hidden, zh=1))]
    pieces[3, 0] = [(0, send(hidden, zh=-1))]
    pieces[0, 1] = [(0, send(hidden, x=1))]
    pieces[0, 3] = [(0, send(hidden, x=-1))]
    pieces[2, 0] = [
        (0, send(pieces[1, 0][0][1][:, :half], zh=1)),
        (half, send(pieces[3, 0][0][1][:, half:], zh=-1)),
    ]
    pieces[0, 2] = [
        (0, send(pieces[0, 1][0][1][:, :half], x=1)),
        (half, send(pieces[0, 3][0][1][:, half:], x=-1)),
    ]
    for dz in (1, 3, 2):
        for dx, step in ((1, 1), (3, -1)):
            pieces[dz, dx] = [(col, send(part, x=step)) for col, part in pieces[dz, 0]]
    left, right = pieces[0, 2][0][1], pieces[0, 2][1][1]
    middle = jnp.concatenate([left[:, a:], right[:, : b - half]], axis=1)
    up = send(middle, zh=1)
    down = send(middle, zh=-1)
    mid = {
        1: [(a, up)],
        3: [(a, down)],
        2: [(a, send(up[:, : half - a], zh=1)), (half, send(down[:, half - a :], zh=-1))],
    }
    for dz in (1, 3, 2):
        first = send(pieces[dz, 1][0][1][:, :a], x=1)
        col, part = pieces[dz, 3][-1]
        last = send(part[:, b - col :], x=-1)
        pieces[dz, 2] = [(0, first)] + mid[dz] + [(b, last)]

    hidden_blocks = hidden.reshape(ex, tok // ex, ff)
    grad_blocks = out_grad.reshape(ex, tok // ex, out_grad.shape[1])
    grams = jnp.stack(
        [
            jnp.einsum("btf,buf->btu", v, v, preferred_element_type=jnp.float32)
            for v in (hidden_blocks, grad_blocks)
        ]
    )
    grams = grams + send(grams, y=2)
    pairs = [(index(*d), index(d[0], d[1], d[2], d[3], d[4] ^ 1)) for d in DEVICES]
    grams = grams + lax.ppermute(grams, ("dp", "tensor"), pairs)
    grams = grams + send(grams, zl=1)
    down_sq = jnp.sum(grams[0] * grams[1], axis=(1, 2))
    weight_count = jnp.float32(D) * jnp.float32(FF)
    clip_factor = jnp.minimum(
        jnp.float32(1.0), jnp.float32(1.0) / jnp.sqrt(down_sq / weight_count + other_sq)
    )
    tile = jnp.broadcast_to(clip_factor[:, None], (ex, 128))
    tile = jnp.stack([tile] + [send(tile, x=d) for d in (1, 2, 3)])
    tile = jnp.stack([tile] + [send(tile, zh=d) for d in (1, 2, 3)])
    clips = tile[:, :, :, 0]

    parts = out_grad.reshape(2, 4, 16, 1024)
    kept, got = pick(parts, zl_at), send(pick(parts, 1 - zl_at), zl=1)
    both = jnp.where(zl_at == 0, jnp.stack([kept, got]), jnp.stack([got, kept]))
    by_y = jnp.swapaxes(both, 0, 1)
    rel = [pick(by_y, y_at)] + [send(pick(by_y, (y_at + d) % 4), y=d) for d in (1, 2, 3)]
    rel = jnp.stack(rel[::-1] + rel[::-1])
    absolute = lax.dynamic_slice_in_dim(rel, (3 - y_at) % 4, 4, 0)
    by_x = absolute.reshape(2, 2, 2, 16, 2, 512)
    by_x = by_x.transpose(1, 4, 2, 0, 3, 5).reshape(4, 4, 16, 512)
    from_x = jnp.stack([pick(by_x, x_at)] + [send(pick(by_x, (x_at + d) % 4), x=d) for d in (1, 2, 3)])
    by_z = jnp.swapaxes(from_x, 0, 1)
    from_z = jnp.stack([pick(by_z, zh_at)] + [send(pick(by_z, (zh_at + d) % 4), zh=d) for d in (1, 2, 3)])
    grad = from_z.reshape(16, 16, 512)
    other = send(grad, zl=1)
    pair = jnp.where(zl_at == 0, jnp.stack([grad, other]), jnp.stack([other, grad]))
    ring = [pair] + [send(pair, y=d) for d in (1, 2, 3)]
    ring = jnp.stack(ring[::-1] + ring[::-1])
    whole = lax.dynamic_slice_in_dim(ring, (3 - y_at) % 4, 4, 0)
    scaled = (clips.reshape(16, 2).T[None, :, :, None, None] * whole.astype(jnp.float32)).astype(
        jnp.bfloat16
    )
    scaled = scaled.transpose(4, 2, 1, 0, 3).reshape(512, 16 * tok)

    flat, layout = [], []
    bounds = (0, a, half, b, ff)
    ids = {}
    for key in [(dz, dx) for dz in range(4) for dx in range(4)]:
        ids[key] = []
        for col, part in pieces[key]:
            ids[key].append((len(flat), col, col + part.shape[1]))
            flat.append(part)
    for lo, hi in zip(bounds[:-1], bounds[1:]):
        blocks = []
        for key in ids:
            blocks += [(p, s) for p, s, e in ids[key] if s <= lo and hi <= e]
        assert len(blocks) == 16
        layout.append((lo, hi, blocks))
    product = pl.pallas_call(
        lambda *refs: matmul_kernel(layout, *refs),
        out_shape=jax.ShapeDtypeStruct((512, ff), jnp.float32),
        in_specs=[pl.BlockSpec(memory_space=pltpu.VMEM)] * (1 + len(flat)),
        out_specs=pl.BlockSpec(memory_space=pltpu.VMEM),
        compiler_params=pltpu.CompilerParams(vmem_limit_bytes=40 << 20),
        cost_estimate=pl.CostEstimate(
            flops=2 * 512 * 2048 * ff, bytes_accessed=12 << 20, transcendentals=0
        ),
    )(scaled, *flat)
    product = product.reshape(2, 256, ff)
    total = pick(product, c_at) + send(pick(product, 1 - c_at), c=1)
    down_grad = total / jnp.float32(examples) + added_noise.astype(jnp.float32)
    return (down_grad, clip_factor)


def solution(mesh):
    in_specs = (P("dp", "tensor"), P("dp", "tensor"), P("dp", "tensor"), P("dp"), P("dp", "tensor"))
    out_specs = (P("dp", "tensor"), P("dp"))
    return jax.shard_map(
        per_device, mesh=mesh, in_specs=in_specs, out_specs=out_specs, check_vma=False
    )
```

```python
import jax
import jax.numpy as jnp
from jax import lax
from jax.experimental import pallas as pl
from jax.experimental.pallas import tpu as pltpu
from jax.sharding import PartitionSpec as P

D = 8192
FF = 14336
TILE = 256

DEVICES = [
    (zh, x, c, zl, y)
    for zh in range(4)
    for x in range(4)
    for c in range(2)
    for zl in range(2)
    for y in range(4)
]


def index(zh, x, c, zl, y):
    return (((zh % 4) * 4 + x % 4) * 2 + c % 2) * 8 + (zl % 2) * 4 + y % 4


def permute(value, to):
    pairs = [(index(*d), index(*to(*d))) for d in DEVICES]
    return lax.ppermute(value, ("dp", "tensor"), pairs)


def send(value, zh=0, x=0, c=0, zl=0, y=0):
    return permute(value, lambda z_, x_, c_, l_, y_: (z_ + zh, x_ + x, c_ + c, l_ + zl, y_ + y))


def pick(stacked, at):
    return lax.dynamic_index_in_dim(stacked, at, 0, keepdims=False)


def product_kernel(pieces, places_ref, clip_ref, *refs):
    n = len(pieces)
    ring_refs, piece_refs, refs = refs[:4], refs[4 : 4 + n], refs[4 + n :]
    theirs_ref, mine_ref, ring, scaled, hidden, acc, ring_sem, sem, out_sem = refs
    copies = [pltpu.make_async_copy(ring_refs[r], ring.at[r], ring_sem.at[r]) for r in range(4)]
    for p, (to, start, rows) in enumerate(pieces):
        copies.append(
            pltpu.make_async_copy(
                piece_refs[p].at[pl.ds(start, rows)], hidden.at[pl.ds(to, rows)], sem.at[p]
            )
        )
    for copy in copies:
        copy.start()
    core, l_at, y_at = places_ref[16], places_ref[17], places_ref[18]
    for copy in copies[:4]:
        copy.wait()
    halves = [pl.ds(pl.multiple_of(h * 256, 256), 256) for h in (1 - core, core)]
    for r in range(4):
        y = (y_at + 4 - r) % 4
        for o in range(2):
            l = l_at if o == 0 else 1 - l_at
            part = (l * 4 + y) * 16

            @pl.loop(0, 16)
            def _(j):
                block = places_ref[j]
                rows = pl.ds(pl.multiple_of(block * 16, 16), 16)
                to = pl.ds(pl.multiple_of(j * 128 + part, 16), 16)
                factor = clip_ref[block * 2 + l]
                for k in range(2):
                    value = ring[r, o, rows, halves[k]].astype(jnp.float32) * factor
                    scaled[to, k * 256 : (k + 1) * 256] = value.astype(jnp.bfloat16)

    for copy in copies[4:]:
        copy.wait()
    outs = []
    for i in range(hidden.shape[1] // TILE):
        at = pl.ds(i * TILE, TILE)
        acc[:, at] = lax.dot_general(
            scaled[...], hidden[:, at], (((0,), (0,)), ((), ())), preferred_element_type=jnp.float32
        )
        for k, out_ref in enumerate((theirs_ref, mine_ref)):
            outs.append(
                pltpu.make_async_copy(
                    acc.at[pl.ds(k * 256, 256), at], out_ref.at[:, at], out_sem.at[k, i]
                )
            )
            outs[-1].start()
    for copy in outs:
        copy.wait()


def pieces_of(h, keys, tok):
    arrays, layout = [], []
    for blk, key in enumerate(keys):
        to = blk * tok
        for array, start, rows in h[key]:
            arrays.append(array)
            layout.append((to, start, rows))
            to += rows
    return arrays, layout


HBM = pl.BlockSpec(memory_space=pltpu.HBM)
VMEM = pl.BlockSpec(memory_space=pltpu.VMEM)
SMEM = pl.BlockSpec(memory_space=pltpu.SMEM)
PARAMS = pltpu.CompilerParams(vmem_limit_bytes=60 << 20)
COST = pl.CostEstimate(flops=1 << 20, bytes_accessed=1 << 20, transcendentals=0)


def product(h, keys, ring, places, clips):
    tok = 128
    arrays, layout = pieces_of(h, keys, tok)
    ff = arrays[0].shape[1]
    return pl.pallas_call(
        lambda *refs: product_kernel(layout, *refs),
        out_shape=[jax.ShapeDtypeStruct((256, ff), jnp.float32)] * 2,
        in_specs=[SMEM, SMEM] + [HBM] * (4 + len(arrays)),
        out_specs=[HBM, HBM],
        scratch_shapes=[
            pltpu.VMEM((4,) + ring[0].shape, jnp.bfloat16),
            pltpu.VMEM((16 * tok, 512), jnp.bfloat16),
            pltpu.VMEM((16 * tok, ff), jnp.bfloat16),
            pltpu.VMEM((512, ff), jnp.float32),
            pltpu.SemaphoreType.DMA((4,)),
            pltpu.SemaphoreType.DMA((len(arrays),)),
            pltpu.SemaphoreType.DMA((2, ff // TILE)),
        ],
        compiler_params=PARAMS,
        cost_estimate=COST,
    )(places, clips, *ring, *arrays)


def split3(value):
    parts = []
    for _ in range(3):
        part = lax.reduce_precision(value, 8, 7)
        parts.append(part.astype(jnp.bfloat16))
        value = value - part
    return parts


def step(inputs, done):
    return lax.optimization_barrier((tuple(inputs), tuple(done)))[0]


def per_device(gate_pre, up_pre, out_grad, other_sq, added_noise):
    dp_at, t_at = lax.axis_index("dp"), lax.axis_index("tensor")
    z_at, x_at, c_at = dp_at // 8, (dp_at // 2) % 4, dp_at % 2
    l_at, y_at = t_at // 4, t_at % 4
    tok, ff = gate_pre.shape
    examples, ex = 64, 2

    def ring_x(value):
        return permute(value, lambda z, x, c, l, y: (z, x + 1 - 2 * c, c, l, y))

    def ring_z(value, way=1):
        return permute(value, lambda z, x, c, l, y: (z + way * (1 - 2 * c), x, c, l, y))

    hidden = (jax.nn.silu(gate_pre.astype(jnp.float32)) * up_pre.astype(jnp.float32)).astype(
        jnp.bfloat16
    )
    hidden_blocks = hidden.reshape(ex, tok // ex, ff)
    grad_blocks = out_grad.reshape(ex, tok // ex, out_grad.shape[1])
    grams = jnp.stack(
        [
            jnp.einsum("btf,buf->btu", v, v, preferred_element_type=jnp.float32)
            for v in (hidden_blocks, grad_blocks)
        ]
    )
    rows = grams.reshape(2, ex, 8, 8, 64).transpose(2, 0, 1, 3, 4).reshape(8, 2, 1024)
    message = jnp.concatenate(
        [out_grad.reshape(8, 16, 1024)] + split3(rows) + [jnp.zeros((8, 2, 1024), jnp.bfloat16)], axis=1
    )

    h = {(0, 0): [(hidden, 0, tok)]}
    z = ring_z(hidden)
    x = ring_x(hidden)
    h[0, 1] = [(x, 0, tok)]
    x = ring_x(x)
    h[1, 0], h[0, 2] = [(z, 0, tok)], [(x, 0, tok)]
    message = lax.all_to_all(message, "tensor", 0, 0, tiled=True)
    x = jnp.concatenate([x, z])
    z, x, message = step((z, x, message), ())
    z = ring_z(z)
    x = ring_x(x)
    h[2, 0], h[0, 3], h[1, 1] = [(z, 0, tok)], [(x, 0, tok)], [(x, tok, tok)]
    rows = jnp.sum(message[:, 16:22].astype(jnp.float32).reshape(8, 3, 2048), axis=(0, 1))
    rows = rows.reshape(2, ex, 8 * 64)
    weight_count = jnp.float32(D) * jnp.float32(FF)
    part = jnp.sum(rows[0] * rows[1], axis=1) / weight_count
    part = part + jnp.where(t_at == 0, other_sq, jnp.zeros_like(other_sq))
    lanes = jnp.repeat(part, 256)[None, :]
    extra = jnp.concatenate(split3(lanes) + [jnp.zeros((5, 512), jnp.bfloat16)])
    own = message[:, :16].reshape(8, 16, 2, 512).transpose(0, 2, 1, 3).reshape(16, 16, 512)
    message = jnp.concatenate([own, jnp.broadcast_to(extra[None], (16, 8, 512))], axis=1)
    groups = [[zx * 2 + c for zx in range(16)] for c in range(2)]
    message = lax.all_to_all(message, "dp", 0, 0, axis_index_groups=groups, tiled=True)
    across = x[:tok]
    x = jnp.concatenate([x[tok:], z])
    z, x, across = step((z, x, across), ())
    z = ring_z(z)
    x = ring_x(x)
    h[3, 0], h[1, 2], h[2, 1] = [(z, 0, tok)], [(x, 0, tok)], [(x, tok, tok)]
    extra = message[:, 16:19].reshape(16, 3, 2, 256)[:, :, :, :64].transpose(0, 2, 1, 3).reshape(16, 384)
    own = jnp.concatenate(
        [message[:, :16].reshape(256, 512), jnp.pad(extra, ((0, 0), (0, 128)))]
    )
    pair = jnp.stack([own, send(own, zl=1)])
    third = x[:tok]
    x = jnp.concatenate([x[tok:], z])
    x, across, pair = step((x, across, pair), ())
    z = ring_z(across, -1)
    x = ring_x(x)
    h[3, 3], h[2, 2], h[3, 1] = [(z, 0, tok)], [(x, 0, tok)], [(x, tok, tok)]
    ring = [pair, send(pair, y=1), None, send(pair, y=3)]
    x = jnp.concatenate([x[tok:], third])
    z, x, pair = step((z, x, pair), (ring[1], ring[3]))
    z = ring_z(z, -1)
    x = ring_x(x)
    h[2, 3], h[3, 2], h[1, 3] = [(z, 0, tok)], [(x, 0, tok)], [(x, tok, tok)]
    ring[2] = send(pair, y=2)

    total = sum(piece[:, 256:].astype(jnp.float32).sum(0) for piece in ring)
    total = total[:, :384].reshape(16, ex, 3, 64)[:, :, :, 0].sum(2)
    clips = jnp.minimum(jnp.float32(1.0), jnp.float32(1.0) / jnp.sqrt(total))
    clip_factor = pick(clips, z_at * 4 + x_at)
    keys = [(dz, dx) for dz in range(4) for dx in range(4)]
    way = 1 - 2 * c_at
    places = [((z_at - way * dz) % 4) * 4 + (x_at - way * dx) % 4 for dz, dx in keys]
    places = jnp.stack(places + [c_at, l_at, y_at])
    theirs, mine = product(h, keys, ring, places, clips.reshape(32))
    total = mine + send(theirs, c=1)
    down_grad = total / jnp.float32(examples) + added_noise.astype(jnp.float32)
    return (down_grad, clip_factor)


def solution(mesh):
    in_specs = (P("dp", "tensor"), P("dp", "tensor"), P("dp", "tensor"), P("dp"), P("dp", "tensor"))
    out_specs = (P("dp", "tensor"), P("dp"))
    return jax.shard_map(
        per_device, mesh=mesh, in_specs=in_specs, out_specs=out_specs, check_vma=False
    )
```

```python
import jax
import jax.numpy as jnp
from jax import lax
from jax.experimental import pallas as pl
from jax.experimental.pallas import tpu as pltpu
from jax.sharding import PartitionSpec as P

D = 8192
FF = 14336
TILE = 896
GROUP = 512

DEVICES = [
    (zh, x, c, zl, y)
    for zh in range(4)
    for x in range(4)
    for c in range(2)
    for zl in range(2)
    for y in range(4)
]


def index(zh, x, c, zl, y):
    return (((zh % 4) * 4 + x % 4) * 2 + c % 2) * 8 + (zl % 2) * 4 + y % 4


def permute(value, to):
    pairs = [(index(*d), index(*to(*d))) for d in DEVICES]
    return lax.ppermute(value, ("dp", "tensor"), pairs)


def send(value, zh=0, x=0, c=0, zl=0, y=0):
    return permute(value, lambda z_, x_, c_, l_, y_: (z_ + zh, x_ + x, c_ + c, l_ + zl, y_ + y))


def pick(stacked, at):
    return lax.dynamic_index_in_dim(stacked, at, 0, keepdims=False)


def product_kernel(pieces, tokens, places_ref, *refs):
    n = len(pieces)
    ring_refs, piece_refs, refs = refs[:4], refs[4 : 4 + n], refs[4 + n + tokens :]
    theirs_ref, mine_ref, ring, factors, scaled, hidden, acc, ring_sem, sem, out_sem = refs
    first = [pltpu.make_async_copy(ring_refs[r], ring.at[r], ring_sem.at[r]) for r in range(4)]
    for copy in first:
        copy.start()
    copies = [
        pltpu.make_async_copy(
            piece_refs[p].at[pl.ds(start, rows)], hidden.at[pl.ds(to, rows)], sem.at[p]
        )
        for p, (to, start, rows) in enumerate(pieces)
    ]
    per = GROUP // 128
    for copy in copies[:per]:
        copy.start()
    core, l_at, y_at = places_ref[16], places_ref[17], places_ref[18]
    for copy in first:
        copy.wait()
    for copy in copies[per : 2 * per]:
        copy.start()
    total = jnp.zeros((16, 512), jnp.float32)
    for r in range(4):
        for o in range(2):
            total += ring[r, o, 256:, :].astype(jnp.float32)
    for l in range(2):
        part = jnp.sum(total[:, l * 256 : (l + 1) * 256], axis=1, keepdims=True) * (1 / 64)
        factor = jnp.minimum(jnp.float32(1.0), jnp.float32(1.0) / jnp.sqrt(part))
        factors[l] = jnp.broadcast_to(factor, (16, 256))
    halves = [pl.ds(pl.multiple_of(h * 256, 256), 256) for h in (1 - core, core)]

    def assemble(j):
        block = places_ref[j]
        rows = pl.ds(pl.multiple_of(block * 16, 16), 16)
        for r in range(4):
            y = (y_at + 4 - r) % 4
            for o in range(2):
                l = l_at if o == 0 else 1 - l_at
                to = pl.ds(pl.multiple_of(j * 128 + (l * 4 + y) * 16, 16), 16)
                factor = factors[l, pl.ds(block, 1), :]
                for k in range(2):
                    value = ring[r, o, rows, halves[k]].astype(jnp.float32) * factor
                    scaled[to, k * 256 : (k + 1) * 256] = value.astype(jnp.bfloat16)

    outs = []
    groups, tiles = hidden.shape[0] // GROUP, hidden.shape[1] // TILE
    for g in range(groups):
        depth = pl.ds(g * GROUP, GROUP)
        for j in range(g * GROUP // 128, (g + 1) * GROUP // 128):
            assemble(j)
        for copy in copies[g * per : (g + 1) * per]:
            copy.wait()
        for copy in copies[(g + 2) * per : (g + 3) * per]:
            copy.start()
        for i in range(tiles):
            at = pl.ds(i * TILE, TILE)
            total = lax.dot_general(
                scaled[depth, :],
                hidden[depth, at],
                (((0,), (0,)), ((), ())),
                preferred_element_type=jnp.float32,
            )
            acc[:, at] = total if g == 0 else acc[:, at] + total
            if g < groups - 1:
                continue
            for k, out_ref in enumerate((theirs_ref, mine_ref)):
                outs.append(
                    pltpu.make_async_copy(
                        acc.at[pl.ds(k * 256, 256), at], out_ref.at[:, at], out_sem.at[k, i]
                    )
                )
                outs[-1].start()
    for copy in outs:
        copy.wait()


def pieces_of(h, keys, tok):
    arrays, layout = [], []
    for blk, key in enumerate(keys):
        to = blk * tok
        for array, start, rows in h[key]:
            arrays.append(array)
            layout.append((to, start, rows))
            to += rows
    return arrays, layout


HBM = pl.BlockSpec(memory_space=pltpu.HBM)
VMEM = pl.BlockSpec(memory_space=pltpu.VMEM)
SMEM = pl.BlockSpec(memory_space=pltpu.SMEM)
PARAMS = pltpu.CompilerParams(vmem_limit_bytes=60 << 20)
COST = pl.CostEstimate(flops=1 << 20, bytes_accessed=1 << 20, transcendentals=0)


def product(h, keys, ring, places, tokens):
    tok = 128
    arrays, layout = pieces_of(h, keys, tok)
    ff = arrays[0].shape[1]
    return pl.pallas_call(
        lambda *refs: product_kernel(layout, len(tokens), *refs),
        out_shape=[jax.ShapeDtypeStruct((256, ff), jnp.float32)] * 2,
        in_specs=[SMEM] + [HBM] * (4 + len(arrays) + len(tokens)),
        out_specs=[HBM, HBM],
        scratch_shapes=[
            pltpu.VMEM((4,) + ring[0].shape, jnp.bfloat16),
            pltpu.VMEM((2, 16, 256), jnp.float32),
            pltpu.VMEM((16 * tok, 512), jnp.bfloat16),
            pltpu.VMEM((16 * tok, ff), jnp.bfloat16),
            pltpu.VMEM((512, ff), jnp.float32),
            pltpu.SemaphoreType.DMA((4,)),
            pltpu.SemaphoreType.DMA((len(arrays),)),
            pltpu.SemaphoreType.DMA((2, ff // TILE)),
        ],
        compiler_params=PARAMS,
        cost_estimate=COST,
    )(places, *ring, *arrays, *tokens)


def split3(value):
    parts = []
    for _ in range(3):
        part = lax.reduce_precision(value, 8, 7)
        parts.append(part.astype(jnp.bfloat16))
        value = value - part
    return parts


def weigh(value, flops):
    def kernel(_, token_ref):
        token_ref[...] = jnp.zeros_like(token_ref)

    return pl.pallas_call(
        kernel,
        out_shape=jax.ShapeDtypeStruct((8, 128), jnp.float32),
        in_specs=[pl.BlockSpec(memory_space=pl.ANY)],
        out_specs=VMEM,
        cost_estimate=pl.CostEstimate(flops=flops, bytes_accessed=1 << 10, transcendentals=0),
    )(value)


def step(inputs, done):
    return lax.optimization_barrier((tuple(inputs), tuple(done)))[0]


def per_device(gate_pre, up_pre, out_grad, other_sq, added_noise):
    dp_at, t_at = lax.axis_index("dp"), lax.axis_index("tensor")
    z_at, x_at, c_at = dp_at // 8, (dp_at // 2) % 4, dp_at % 2
    l_at, y_at = t_at // 4, t_at % 4
    tok, ff = gate_pre.shape
    examples, ex = 64, 2

    def ring_x(value):
        return permute(value, lambda z, x, c, l, y: (z, x + 1 - 2 * c, c, l, y))

    def ring_z(value, way=1):
        return permute(value, lambda z, x, c, l, y: (z + way * (1 - 2 * c), x, c, l, y))

    hidden = (jax.nn.silu(gate_pre.astype(jnp.float32)) * up_pre.astype(jnp.float32)).astype(
        jnp.bfloat16
    )
    hidden_blocks = hidden.reshape(ex, tok // ex, ff)
    grad_blocks = out_grad.reshape(ex, tok // ex, out_grad.shape[1])
    grams = jnp.stack(
        [
            jnp.einsum("btf,buf->btu", v, v, preferred_element_type=jnp.float32)
            for v in (hidden_blocks, grad_blocks)
        ]
    )
    rows = grams.reshape(2, ex, 8, 8, 64).transpose(2, 0, 1, 3, 4).reshape(8, 2, 1024)
    message = jnp.concatenate(
        [out_grad.reshape(8, 16, 1024)] + split3(rows) + [jnp.zeros((8, 2, 1024), jnp.bfloat16)], axis=1
    )

    h = {(0, 0): [(hidden, 0, tok)]}
    z = ring_z(hidden)
    x = ring_x(hidden)
    h[0, 1] = [(x, 0, tok)]
    x = ring_x(x)
    h[1, 0], h[0, 2] = [(z, 0, tok)], [(x, 0, tok)]
    message = lax.all_to_all(message, "tensor", 0, 0, tiled=True)
    z, x, x2, message, tz0 = step((z, x, z, message, weigh(z, 10737418240)), ())
    z = ring_z(z)
    across = ring_x(x)
    x = ring_x(x2)
    h[2, 0], h[0, 3], h[1, 1] = [(z, 0, tok)], [(across, 0, tok)], [(x, 0, tok)]
    message, across = step((message, across), ())
    rows = jnp.sum(message[:, 16:22].astype(jnp.float32).reshape(8, 3, 2048), axis=(0, 1))
    rows = rows.reshape(2, ex, 8 * 64)
    weight_count = jnp.float32(D) * jnp.float32(FF)
    part = jnp.sum(rows[0] * rows[1], axis=1) / weight_count
    part = part + jnp.where(t_at == 0, other_sq, jnp.zeros_like(other_sq))
    lanes = jnp.repeat(part, 256)[None, :]
    extra = jnp.concatenate(split3(lanes) + [jnp.zeros((5, 512), jnp.bfloat16)])
    own = message[:, :16].reshape(8, 16, 2, 512).transpose(0, 2, 1, 3).reshape(16, 16, 512)
    message = jnp.concatenate([own, jnp.broadcast_to(extra[None], (16, 8, 512))], axis=1)
    groups = [[zx * 2 + c for zx in range(16)] for c in range(2)]
    message = lax.all_to_all(message, "dp", 0, 0, axis_index_groups=groups, tiled=True)
    x = jnp.concatenate([x, z])
    z, x, across = step((z, x, across), ())
    z = ring_z(z)
    x = ring_x(x)
    h[3, 0], h[1, 2], h[2, 1] = [(z, 0, tok)], [(x, 0, tok)], [(x, tok, tok)]
    extra = message[:, 16:19].reshape(16, 3, 2, 256)[:, :, :, :64].transpose(0, 2, 1, 3)
    extra = jnp.pad(extra, ((0, 0), (0, 0), (0, 1), (0, 0))).reshape(16, 512)
    own = jnp.concatenate([message[:, :16].reshape(256, 512), extra])
    pair = jnp.stack([own, send(own, zl=1)])
    third = x[:tok]
    x = jnp.concatenate([x[tok:], z])
    x, across, pair = step((x, across, pair), ())
    z = ring_z(across, -1)
    x = ring_x(x)
    h[3, 3], h[2, 2], h[3, 1] = [(z, 0, tok)], [(x, 0, tok)], [(x, tok, tok)]
    ring = [pair, send(pair, y=1), None, send(pair, y=3)]
    x = jnp.concatenate([x[tok:], third])
    z, x, pair, ring[1], ring[3] = step((z, x, pair, ring[1], ring[3]), ())
    z = ring_z(z, -1)
    x = ring_x(x)
    h[2, 3], h[3, 2], h[1, 3] = [(z, 0, tok)], [(x, 0, tok)], [(x, tok, tok)]
    ring[2] = send(pair, y=2)

    total = sum(piece[:, 256:].astype(jnp.float32).sum(0) for piece in ring)
    total = total.reshape(16, ex, 4, 64)[:, :, :, 0].sum(2)
    clips = jnp.minimum(jnp.float32(1.0), jnp.float32(1.0) / jnp.sqrt(total))
    clip_factor = pick(clips, z_at * 4 + x_at)
    keys = [(dz, dx) for dz in range(4) for dx in range(4)]
    way = 1 - 2 * c_at
    places = [((z_at - way * dz) % 4) * 4 + (x_at - way * dx) % 4 for dz, dx in keys]
    places = jnp.stack(places + [c_at, l_at, y_at])
    theirs, mine = product(h, keys, ring, places, [tz0])
    total = mine + send(theirs, c=1)
    down_grad = total / jnp.float32(examples) + added_noise.astype(jnp.float32)
    return (down_grad, clip_factor)


def solution(mesh):
    in_specs = (P("dp", "tensor"), P("dp", "tensor"), P("dp", "tensor"), P("dp"), P("dp", "tensor"))
    out_specs = (P("dp", "tensor"), P("dp"))
    return jax.shard_map(
        per_device, mesh=mesh, in_specs=in_specs, out_specs=out_specs, check_vma=False
    )
```

```python
import jax
import jax.numpy as jnp
from jax import lax
from jax.experimental import pallas as pl
from jax.experimental.pallas import tpu as pltpu
from jax.sharding import PartitionSpec as P

D = 8192
FF = 14336
TILE = 896
GROUP = 512

DEVICES = [
    (zh, x, c, zl, y)
    for zh in range(4)
    for x in range(4)
    for c in range(2)
    for zl in range(2)
    for y in range(4)
]


def index(zh, x, c, zl, y):
    return (((zh % 4) * 4 + x % 4) * 2 + c % 2) * 8 + (zl % 2) * 4 + y % 4


def permute(value, to):
    pairs = [(index(*d), index(*to(*d))) for d in DEVICES]
    return lax.ppermute(value, ("dp", "tensor"), pairs)


def send(value, zh=0, x=0, c=0, zl=0, y=0):
    return permute(value, lambda z_, x_, c_, l_, y_: (z_ + zh, x_ + x, c_ + c, l_ + zl, y_ + y))


def pick(stacked, at):
    return lax.dynamic_index_in_dim(stacked, at, 0, keepdims=False)


def product_kernel(pieces, tokens, places_ref, *refs):
    n = len(pieces)
    ring_refs, piece_refs, refs = refs[:4], refs[4 : 4 + n], refs[4 + n + tokens :]
    theirs_ref, mine_ref, ring, factors, scaled, hidden, acc, ring_sem, sem, out_sem = refs
    first = [pltpu.make_async_copy(ring_refs[r], ring.at[r], ring_sem.at[r]) for r in range(4)]
    for copy in first:
        copy.start()
    copies = [
        pltpu.make_async_copy(
            piece_refs[p].at[pl.ds(start, rows)], hidden.at[pl.ds(to, rows)], sem.at[p]
        )
        for p, (to, start, rows) in enumerate(pieces)
    ]
    per = GROUP // 128
    for copy in copies[:per]:
        copy.start()
    core, l_at, y_at = places_ref[16], places_ref[17], places_ref[18]
    for copy in first:
        copy.wait()
    for copy in copies[per : 2 * per]:
        copy.start()
    total = jnp.zeros((16, 512), jnp.float32)
    for r in range(4):
        for o in range(2):
            total += ring[r, o, 256:, :].astype(jnp.float32)
    for l in range(2):
        part = jnp.sum(total[:, l * 256 : (l + 1) * 256], axis=1, keepdims=True) * (1 / 64)
        factor = jnp.minimum(jnp.float32(1.0), jnp.float32(1.0) / jnp.sqrt(part))
        factors[l] = jnp.broadcast_to(factor, (16, 256))
    halves = [pl.ds(pl.multiple_of(h * 256, 256), 256) for h in (1 - core, core)]

    def assemble(j):
        block = places_ref[j]
        rows = pl.ds(pl.multiple_of(block * 16, 16), 16)
        for r in range(4):
            y = (y_at + 4 - r) % 4
            for o in range(2):
                l = l_at if o == 0 else 1 - l_at
                to = pl.ds(pl.multiple_of(j * 128 + (l * 4 + y) * 16, 16), 16)
                factor = factors[l, pl.ds(block, 1), :]
                for k in range(2):
                    value = ring[r, o, rows, halves[k]].astype(jnp.float32) * factor
                    scaled[to, k * 256 : (k + 1) * 256] = value.astype(jnp.bfloat16)

    outs = []
    groups, tiles = hidden.shape[0] // GROUP, hidden.shape[1] // TILE
    for g in range(groups):
        depth = pl.ds(g * GROUP, GROUP)
        for j in range(g * GROUP // 128, (g + 1) * GROUP // 128):
            assemble(j)
        for copy in copies[g * per : (g + 1) * per]:
            copy.wait()
        for copy in copies[(g + 2) * per : (g + 3) * per]:
            copy.start()
        for i in range(tiles):
            at = pl.ds(i * TILE, TILE)
            total = lax.dot_general(
                scaled[depth, :],
                hidden[depth, at],
                (((0,), (0,)), ((), ())),
                preferred_element_type=jnp.float32,
            )
            acc[:, at] = total if g == 0 else acc[:, at] + total
            if g < groups - 1:
                continue
            for k, out_ref in enumerate((theirs_ref, mine_ref)):
                outs.append(
                    pltpu.make_async_copy(
                        acc.at[pl.ds(k * 256, 256), at], out_ref.at[:, at], out_sem.at[k, i]
                    )
                )
                outs[-1].start()
    for copy in outs:
        copy.wait()


def pieces_of(h, keys, tok):
    arrays, layout = [], []
    for blk, key in enumerate(keys):
        to = blk * tok
        for array, start, rows in h[key]:
            arrays.append(array)
            layout.append((to, start, rows))
            to += rows
    return arrays, layout


HBM = pl.BlockSpec(memory_space=pltpu.HBM)
VMEM = pl.BlockSpec(memory_space=pltpu.VMEM)
SMEM = pl.BlockSpec(memory_space=pltpu.SMEM)
PARAMS = pltpu.CompilerParams(vmem_limit_bytes=60 << 20)
COST = pl.CostEstimate(flops=1 << 20, bytes_accessed=1 << 20, transcendentals=0)


def product(h, keys, ring, places, tokens):
    tok = 128
    arrays, layout = pieces_of(h, keys, tok)
    ff = arrays[0].shape[1]
    return pl.pallas_call(
        lambda *refs: product_kernel(layout, len(tokens), *refs),
        out_shape=[jax.ShapeDtypeStruct((256, ff), jnp.float32)] * 2,
        in_specs=[SMEM] + [HBM] * (4 + len(arrays) + len(tokens)),
        out_specs=[HBM, HBM],
        scratch_shapes=[
            pltpu.VMEM((4,) + ring[0].shape, jnp.bfloat16),
            pltpu.VMEM((2, 16, 256), jnp.float32),
            pltpu.VMEM((16 * tok, 512), jnp.bfloat16),
            pltpu.VMEM((16 * tok, ff), jnp.bfloat16),
            pltpu.VMEM((512, ff), jnp.float32),
            pltpu.SemaphoreType.DMA((4,)),
            pltpu.SemaphoreType.DMA((len(arrays),)),
            pltpu.SemaphoreType.DMA((2, ff // TILE)),
        ],
        compiler_params=PARAMS,
        cost_estimate=COST,
    )(places, *ring, *arrays, *tokens)


def split3(value):
    parts = []
    for _ in range(3):
        part = lax.reduce_precision(value, 8, 7)
        parts.append(part.astype(jnp.bfloat16))
        value = value - part
    return parts


def weigh(value, flops):
    def kernel(_, token_ref):
        token_ref[...] = jnp.zeros_like(token_ref)

    return pl.pallas_call(
        kernel,
        out_shape=jax.ShapeDtypeStruct((8, 128), jnp.float32),
        in_specs=[pl.BlockSpec(memory_space=pl.ANY)],
        out_specs=VMEM,
        cost_estimate=pl.CostEstimate(flops=flops, bytes_accessed=1 << 10, transcendentals=0),
    )(value)


def step(inputs, done):
    return lax.optimization_barrier((tuple(inputs), tuple(done)))[0]


def per_device(gate_pre, up_pre, out_grad, other_sq, added_noise):
    dp_at, t_at = lax.axis_index("dp"), lax.axis_index("tensor")
    z_at, x_at, c_at = dp_at // 8, (dp_at // 2) % 4, dp_at % 2
    l_at, y_at = t_at // 4, t_at % 4
    tok, ff = gate_pre.shape
    examples, ex = 64, 2

    def ring_x(value):
        return permute(value, lambda z, x, c, l, y: (z, x + 1 - 2 * c, c, l, y))

    def ring_z(value, way=1):
        return permute(value, lambda z, x, c, l, y: (z + way * (1 - 2 * c), x, c, l, y))

    hidden = (jax.nn.silu(gate_pre.astype(jnp.float32)) * up_pre.astype(jnp.float32)).astype(
        jnp.bfloat16
    )
    hidden_blocks = hidden.reshape(ex, tok // ex, ff)
    grad_blocks = out_grad.reshape(ex, tok // ex, out_grad.shape[1])
    grams = jnp.stack(
        [
            jnp.einsum("btf,buf->btu", v, v, preferred_element_type=jnp.float32)
            for v in (hidden_blocks, grad_blocks)
        ]
    )
    rows = grams.reshape(2, ex, 8, 8, 64).transpose(2, 0, 1, 3, 4).reshape(8, 2, 1024)
    rows = jnp.concatenate(split3(rows) + [jnp.zeros((8, 2, 1024), jnp.bfloat16)], axis=1)
    rows = step((rows,), ())[0]
    message = jnp.concatenate([out_grad.reshape(8, 16, 1024), rows], axis=1)

    h = {(0, 0): [(hidden, 0, tok)]}
    z = ring_z(hidden)
    x = ring_x(hidden)
    h[0, 1] = [(x, 0, tok)]
    x = ring_x(x)
    h[1, 0], h[0, 2] = [(z, 0, tok)], [(x, 0, tok)]
    message = lax.all_to_all(message, "tensor", 0, 0, tiled=True)
    z, x, x2, message, tz0 = step((z, x, z, message, weigh(z, 10737418240)), ())
    z = ring_z(z)
    across = ring_x(x)
    x = ring_x(x2)
    h[2, 0], h[0, 3], h[1, 1] = [(z, 0, tok)], [(across, 0, tok)], [(x, 0, tok)]
    message, across = step((message, across), ())
    rows = jnp.sum(message[:, 16:22].astype(jnp.float32).reshape(8, 3, 2048), axis=(0, 1))
    rows = rows.reshape(2, ex, 8 * 64)
    weight_count = jnp.float32(D) * jnp.float32(FF)
    part = jnp.sum(rows[0] * rows[1], axis=1) / weight_count
    part = part + jnp.where(t_at == 0, other_sq, jnp.zeros_like(other_sq))
    lanes = jnp.repeat(part, 256)[None, :]
    extra = jnp.concatenate(split3(lanes) + [jnp.zeros((5, 512), jnp.bfloat16)])
    own = message[:, :16].reshape(8, 16, 2, 512).transpose(0, 2, 1, 3).reshape(16, 16, 512)
    message = jnp.concatenate([own, jnp.broadcast_to(extra[None], (16, 8, 512))], axis=1)
    groups = [[zx * 2 + c for zx in range(16)] for c in range(2)]
    message = lax.all_to_all(message, "dp", 0, 0, axis_index_groups=groups, tiled=True)
    x = jnp.concatenate([x, z])
    z, x, across = step((z, x, across), ())
    z = ring_z(z)
    x = ring_x(x)
    h[3, 0], h[1, 2], h[2, 1] = [(z, 0, tok)], [(x, 0, tok)], [(x, tok, tok)]
    extra = message[:, 16:19].reshape(16, 3, 2, 256)[:, :, :, :64].transpose(0, 2, 1, 3)
    extra = jnp.pad(extra, ((0, 0), (0, 0), (0, 1), (0, 0))).reshape(16, 512)
    own = jnp.concatenate([message[:, :16].reshape(256, 512), extra])
    pair = jnp.stack([own, send(own, zl=1)])
    third = x[:tok]
    x = jnp.concatenate([x[tok:], z])
    x, across, pair = step((x, across, pair), ())
    z = ring_z(across, -1)
    x = ring_x(x)
    h[3, 3], h[2, 2], h[3, 1] = [(z, 0, tok)], [(x, 0, tok)], [(x, tok, tok)]
    ring = [pair, send(pair, y=1), None, send(pair, y=3)]
    x = jnp.concatenate([x[tok:], third])
    z, x, pair, ring[1], ring[3] = step((z, x, pair, ring[1], ring[3]), ())
    z = ring_z(z, -1)
    x = ring_x(x)
    h[2, 3], h[3, 2], h[1, 3] = [(z, 0, tok)], [(x, 0, tok)], [(x, tok, tok)]
    tz4 = weigh(z, 3 << 30)
    ring[2] = send(pair, y=2)

    total = sum(piece[:, 256:].astype(jnp.float32).sum(0) for piece in ring)
    total = total.reshape(16, ex, 4, 64)[:, :, :, 0].sum(2)
    clips = jnp.minimum(jnp.float32(1.0), jnp.float32(1.0) / jnp.sqrt(total))
    clip_factor = pick(clips, z_at * 4 + x_at)
    keys = [(dz, dx) for dz in range(4) for dx in range(4)]
    way = 1 - 2 * c_at
    places = [((z_at - way * dz) % 4) * 4 + (x_at - way * dx) % 4 for dz, dx in keys]
    places = jnp.stack(places + [c_at, l_at, y_at])
    theirs, mine = product(h, keys, ring, places, [tz0, tz4])
    total = mine + send(theirs, c=1)
    down_grad = total / jnp.float32(examples) + added_noise.astype(jnp.float32)
    return (down_grad, clip_factor)


def solution(mesh):
    in_specs = (P("dp", "tensor"), P("dp", "tensor"), P("dp", "tensor"), P("dp"), P("dp", "tensor"))
    out_specs = (P("dp", "tensor"), P("dp"))
    return jax.shard_map(
        per_device, mesh=mesh, in_specs=in_specs, out_specs=out_specs, check_vma=False
    )
```

```python
import jax
import jax.numpy as jnp
from jax import lax
from jax.experimental import pallas as pl
from jax.experimental.pallas import tpu as pltpu
from jax.sharding import PartitionSpec as P

D = 8192
FF = 14336
TILE = 256
GROUP = 1024

DEVICES = [
    (zh, x, c, zl, y)
    for zh in range(4)
    for x in range(4)
    for c in range(2)
    for zl in range(2)
    for y in range(4)
]


def index(zh, x, c, zl, y):
    return (((zh % 4) * 4 + x % 4) * 2 + c % 2) * 8 + (zl % 2) * 4 + y % 4


def permute(value, to):
    pairs = [(index(*d), index(*to(*d))) for d in DEVICES]
    return lax.ppermute(value, ("dp", "tensor"), pairs)


def send(value, zh=0, x=0, c=0, zl=0, y=0):
    return permute(value, lambda z_, x_, c_, l_, y_: (z_ + zh, x_ + x, c_ + c, l_ + zl, y_ + y))


def pick(stacked, at):
    return lax.dynamic_index_in_dim(stacked, at, 0, keepdims=False)


def product_kernel(pieces, tokens, places_ref, *refs):
    n = len(pieces)
    ring_refs, piece_refs, refs = refs[:4], refs[4 : 4 + n], refs[4 + n + tokens :]
    theirs_ref, mine_ref, ring, factors, scaled, hidden, acc, ring_sem, sem, out_sem = refs
    first = [pltpu.make_async_copy(ring_refs[r], ring.at[r], ring_sem.at[r]) for r in range(4)]
    for copy in first:
        copy.start()
    copies = [
        pltpu.make_async_copy(
            piece_refs[p].at[pl.ds(start, rows)], hidden.at[pl.ds(to, rows)], sem.at[p]
        )
        for p, (to, start, rows) in enumerate(pieces)
    ]
    per = GROUP // 128
    for copy in copies[:per]:
        copy.start()
    core, l_at, y_at = places_ref[16], places_ref[17], places_ref[18]
    for copy in first:
        copy.wait()
    for copy in copies[per : 2 * per]:
        copy.start()
    total = jnp.zeros((16, 512), jnp.float32)
    for r in range(4):
        for o in range(2):
            total += ring[r, o, 256:, :].astype(jnp.float32)
    for l in range(2):
        part = jnp.sum(total[:, l * 256 : (l + 1) * 256], axis=1, keepdims=True) * (1 / 64)
        factor = jnp.minimum(jnp.float32(1.0), jnp.float32(1.0) / jnp.sqrt(part))
        factors[l] = jnp.broadcast_to(factor, (16, 256))
    halves = [pl.ds(pl.multiple_of(h * 256, 256), 256) for h in (1 - core, core)]

    def assemble(j):
        block = places_ref[j]
        rows = pl.ds(pl.multiple_of(block * 16, 16), 16)
        for r in range(4):
            y = (y_at + 4 - r) % 4
            for o in range(2):
                l = l_at if o == 0 else 1 - l_at
                to = pl.ds(pl.multiple_of(j * 128 + (l * 4 + y) * 16, 16), 16)
                factor = factors[l, pl.ds(block, 1), :]
                for k in range(2):
                    value = ring[r, o, rows, halves[k]].astype(jnp.float32) * factor
                    scaled[to, k * 256 : (k + 1) * 256] = value.astype(jnp.bfloat16)

    outs = []
    groups, tiles = hidden.shape[0] // GROUP, hidden.shape[1] // TILE
    for g in range(groups):
        depth = pl.ds(g * GROUP, GROUP)
        for j in range(g * GROUP // 128, (g + 1) * GROUP // 128):
            assemble(j)
        for copy in copies[g * per : (g + 1) * per]:
            copy.wait()
        for copy in copies[(g + 2) * per : (g + 3) * per]:
            copy.start()
        for i in range(tiles):
            at = pl.ds(i * TILE, TILE)
            total = lax.dot_general(
                scaled[depth, :],
                hidden[depth, at],
                (((0,), (0,)), ((), ())),
                preferred_element_type=jnp.float32,
            )
            acc[:, at] = total if g == 0 else acc[:, at] + total
            if g < groups - 1:
                continue
            for k, out_ref in enumerate((theirs_ref, mine_ref)):
                outs.append(
                    pltpu.make_async_copy(
                        acc.at[pl.ds(k * 256, 256), at], out_ref.at[:, at], out_sem.at[k, i]
                    )
                )
                outs[-1].start()
    for copy in outs:
        copy.wait()


def pieces_of(h, keys, tok):
    arrays, layout = [], []
    for blk, key in enumerate(keys):
        to = blk * tok
        for array, start, rows in h[key]:
            arrays.append(array)
            layout.append((to, start, rows))
            to += rows
    return arrays, layout


HBM = pl.BlockSpec(memory_space=pltpu.HBM)
VMEM = pl.BlockSpec(memory_space=pltpu.VMEM)
SMEM = pl.BlockSpec(memory_space=pltpu.SMEM)
PARAMS = pltpu.CompilerParams(vmem_limit_bytes=60 << 20)
COST = pl.CostEstimate(flops=1 << 20, bytes_accessed=1 << 20, transcendentals=0)


def product(h, keys, ring, places, tokens):
    tok = 128
    arrays, layout = pieces_of(h, keys, tok)
    ff = arrays[0].shape[1]
    return pl.pallas_call(
        lambda *refs: product_kernel(layout, len(tokens), *refs),
        out_shape=[jax.ShapeDtypeStruct((256, ff), jnp.float32)] * 2,
        in_specs=[SMEM] + [HBM] * (4 + len(arrays) + len(tokens)),
        out_specs=[HBM, HBM],
        scratch_shapes=[
            pltpu.VMEM((4,) + ring[0].shape, jnp.bfloat16),
            pltpu.VMEM((2, 16, 256), jnp.float32),
            pltpu.VMEM((16 * tok, 512), jnp.bfloat16),
            pltpu.VMEM((16 * tok, ff), jnp.bfloat16),
            pltpu.VMEM((512, ff), jnp.float32),
            pltpu.SemaphoreType.DMA((4,)),
            pltpu.SemaphoreType.DMA((len(arrays),)),
            pltpu.SemaphoreType.DMA((2, ff // TILE)),
        ],
        compiler_params=PARAMS,
        cost_estimate=COST,
    )(places, *ring, *arrays, *tokens)


def split3(value):
    parts = []
    for _ in range(3):
        part = lax.reduce_precision(value, 8, 7)
        parts.append(part.astype(jnp.bfloat16))
        value = value - part
    return parts


def weigh(value, flops):
    def kernel(_, token_ref):
        token_ref[...] = jnp.zeros_like(token_ref)

    return pl.pallas_call(
        kernel,
        out_shape=jax.ShapeDtypeStruct((8, 128), jnp.float32),
        in_specs=[pl.BlockSpec(memory_space=pl.ANY)],
        out_specs=VMEM,
        cost_estimate=pl.CostEstimate(flops=flops, bytes_accessed=1 << 10, transcendentals=0),
    )(value)


def step(inputs, done):
    return lax.optimization_barrier((tuple(inputs), tuple(done)))[0]


def per_device(gate_pre, up_pre, out_grad, other_sq, added_noise):
    dp_at, t_at = lax.axis_index("dp"), lax.axis_index("tensor")
    z_at, x_at, c_at = dp_at // 8, (dp_at // 2) % 4, dp_at % 2
    l_at, y_at = t_at // 4, t_at % 4
    tok, ff = gate_pre.shape
    examples, ex = 64, 2

    def ring_x(value):
        return permute(value, lambda z, x, c, l, y: (z, x + 1 - 2 * c, c, l, y))

    def ring_z(value, way=1):
        return permute(value, lambda z, x, c, l, y: (z + way * (1 - 2 * c), x, c, l, y))

    hidden = (jax.nn.silu(gate_pre.astype(jnp.float32)) * up_pre.astype(jnp.float32)).astype(
        jnp.bfloat16
    )
    hidden_blocks = hidden.reshape(ex, tok // ex, ff)
    grad_blocks = out_grad.reshape(ex, tok // ex, out_grad.shape[1])
    grams = jnp.stack(
        [
            jnp.einsum("btf,buf->btu", v, v, preferred_element_type=jnp.float32)
            for v in (hidden_blocks, grad_blocks)
        ]
    )
    rows = grams.reshape(2, ex, 8, 8, 64).transpose(2, 0, 1, 3, 4).reshape(8, 2, 1024)
    rows = jnp.concatenate(split3(rows) + [jnp.zeros((8, 2, 1024), jnp.bfloat16)], axis=1)
    rows = step((rows,), ())[0]
    message = jnp.concatenate([out_grad.reshape(8, 16, 1024), rows], axis=1)

    h = {(0, 0): [(hidden, 0, tok)]}
    z = ring_z(hidden)
    x = ring_x(hidden)
    h[0, 1] = [(x, 0, tok)]
    x = ring_x(x)
    h[1, 0], h[0, 2] = [(z, 0, tok)], [(x, 0, tok)]
    message = lax.all_to_all(message, "tensor", 0, 0, tiled=True)
    z, x, x2, message, tz0 = step((z, x, z, message, weigh(z, 10737418240)), ())
    z = ring_z(z)
    across = ring_x(x)
    x = ring_x(x2)
    h[2, 0], h[0, 3], h[1, 1] = [(z, 0, tok)], [(across, 0, tok)], [(x, 0, tok)]
    message, across = step((message, across), ())
    rows = jnp.sum(message[:, 16:22].astype(jnp.float32).reshape(8, 3, 2048), axis=(0, 1))
    rows = rows.reshape(2, ex, 8 * 64)
    weight_count = jnp.float32(D) * jnp.float32(FF)
    part = jnp.sum(rows[0] * rows[1], axis=1) / weight_count
    part = part + jnp.where(t_at == 0, other_sq, jnp.zeros_like(other_sq))
    lanes = jnp.repeat(part, 256)[None, :]
    extra = jnp.concatenate(split3(lanes) + [jnp.zeros((5, 512), jnp.bfloat16)])
    own = message[:, :16].reshape(8, 16, 2, 512).transpose(0, 2, 1, 3).reshape(16, 16, 512)
    message = jnp.concatenate([own, jnp.broadcast_to(extra[None], (16, 8, 512))], axis=1)
    groups = [[zx * 2 + c for zx in range(16)] for c in range(2)]
    message = lax.all_to_all(message, "dp", 0, 0, axis_index_groups=groups, tiled=True)
    x = jnp.concatenate([x, z])
    z, x, across = step((z, x, across), ())
    z = ring_z(z)
    x = ring_x(x)
    h[3, 0], h[1, 2], h[2, 1] = [(z, 0, tok)], [(x, 0, tok)], [(x, tok, tok)]
    extra = message[:, 16:19].reshape(16, 3, 2, 256)[:, :, :, :64].transpose(0, 2, 1, 3)
    extra = jnp.pad(extra, ((0, 0), (0, 0), (0, 1), (0, 0))).reshape(16, 512)
    own = jnp.concatenate([message[:, :16].reshape(256, 512), extra])
    pair = jnp.stack([own, send(own, zl=1)])
    third = x[:tok]
    x = jnp.concatenate([x[tok:], z])
    x, across, pair = step((x, across, pair), ())
    z = ring_z(across, -1)
    x = ring_x(x)
    h[3, 3], h[2, 2], h[3, 1] = [(z, 0, tok)], [(x, 0, tok)], [(x, tok, tok)]
    ring = [pair, send(pair, y=1), None, send(pair, y=3)]
    x = jnp.concatenate([x[tok:], third])
    z, x, pair, ring[1], ring[3] = step((z, x, pair, ring[1], ring[3]), ())
    z = ring_z(z, -1)
    x = ring_x(x)
    h[2, 3], h[3, 2], h[1, 3] = [(z, 0, tok)], [(x, 0, tok)], [(x, tok, tok)]
    tz4 = weigh(z, 3 << 30)
    ring[2] = send(pair, y=2)

    total = sum(piece[:, 256:].astype(jnp.float32).sum(0) for piece in ring)
    total = total.reshape(16, ex, 4, 64)[:, :, :, 0].sum(2)
    clips = jnp.minimum(jnp.float32(1.0), jnp.float32(1.0) / jnp.sqrt(total))
    clip_factor = pick(clips, z_at * 4 + x_at)
    keys = [(dz, dx) for dz in range(4) for dx in range(4)]
    way = 1 - 2 * c_at
    places = [((z_at - way * dz) % 4) * 4 + (x_at - way * dx) % 4 for dz, dx in keys]
    places = jnp.stack(places + [c_at, l_at, y_at])
    theirs, mine = product(h, keys, ring, places, [tz0, tz4])
    total = mine + send(theirs, c=1)
    down_grad = total / jnp.float32(examples) + added_noise.astype(jnp.float32)
    return (down_grad, clip_factor)


def solution(mesh):
    in_specs = (P("dp", "tensor"), P("dp", "tensor"), P("dp", "tensor"), P("dp"), P("dp", "tensor"))
    out_specs = (P("dp", "tensor"), P("dp"))
    return jax.shard_map(
        per_device, mesh=mesh, in_specs=in_specs, out_specs=out_specs, check_vma=False
    )
```
